32 devices in a mesh: groups: 2 (over y), wide: 8 (over z, core), narrow: 2 (over x).
Axes of the slice: x: 2, y: 2, z: 4, core: 2. Of those that a mesh axis runs over, the one named last changes fastest.
Arguments:
- blocks: bfloat16 [64, 128, 128, 128], P(('groups', 'wide'), None, 'narrow'), parts along dimension 0, may hold values from -6 to 6
- occupied: bfloat16 [16, 512, 512], P('groups', ('wide', 'narrow')), parts along dimension 0, may hold values from -0.5 to 0.5
- virtual: bfloat16 [16, 512, 512], P('groups', ('wide', 'narrow')), parts along dimension 0, may hold values from -0.5 to 0.5
- item_mu: int32 [64], P(('groups', 'wide')), parts along dimension 0, may hold values from 0 to 3
- item_nu: int32 [64], P(('groups', 'wide')), parts along dimension 0, may hold values from 0 to 3
- item_target: int32 [64], P(('groups', 'wide')), parts along dimension 0, may hold values from 0 to 15
- live_counts: int32 [16], P(('groups', 'wide')), parts along dimension 0, may hold values from 1 to 4, 21 in all
- target_occ: int32 [32], P('groups'), parts along dimension 0, may hold values from 0 to 3
- target_virt: int32 [32], P('groups'), parts along dimension 0, may hold values from 0 to 3
Outputs:
- transformed: bfloat16 [16, 16, 128, 128, 128], P('groups', None, 'wide', 'narrow'), parts along dimension 0
The draws below stay inside these ranges and needn't reach their ends.
There are 2 independent parts, one for each index of `groups`. The reference program is written for one: setup_inputs(seed, part) draws one part's arguments, and reference() takes and returns one part's arrays. A program takes and returns all parts, laid end to end along the dimension named above; each array names one. Nothing has to cross between parts.
Inputs may be any that keep to these rules, and one draw needn't show every extreme that they name: The first live_counts[w] of the 4 slots of index w of wide are live; the counts sum to 21 and the largest is 4.
All inputs are finite; a program needn't handle non-finite values. No bound on the sum of `live_counts` on one device may be relied on, other than what follows from the above.
Results may differ from the reference program's by a relative error of at most 0.005.
Values may be sent and summed in bfloat16 or wider, within the bound.
A program may use at most 640 MiB of HBM per device.

```python
import math
import jax
import jax.numpy as jnp
import numpy as np
from jax import lax

BA = 128
BO = 128
NB = 4
NTAU = 8
SLOTS = 4
NT = 16
NITEMS = 32
LIVE_TOTAL = 21
NO = 512
N_WIDE = 8


def place_ends(drawn, stream_key, least, largest):
    longest = drawn.shape.index(max(drawn.shape))
    spots = []
    for shift in (0, 1):
        where = [jax.random.randint(jax.random.fold_in(stream_key, axis), (), 0, length) for axis, length in enumerate(drawn.shape)]
        where[longest] = (where[longest] + shift) % drawn.shape[longest]
        spots.append(tuple(where))
    return drawn.at[spots[0]].set(least).at[spots[1]].set(largest)


def levels(key, shape, split, low, high):
    factor_of = 1.0
    for axis_at, blocks in split:
        draws = jax.random.uniform(jax.random.fold_in(jax.random.fold_in(key, 6), axis_at), (blocks,), jnp.float32, low / len(split), high / len(split))
        factor_of = factor_of * jnp.repeat(jnp.exp(draws), shape[axis_at] // blocks).reshape((-1,) + (1,) * (len(shape) - 1 - axis_at))
    return factor_of


def profile(amount, total, limit, slope):
    loads = [(1 << 20) // math.isqrt(grade ** slope) + 1 for grade in range(2, amount + 1)]
    surplus, counts = total - limit - (amount - 1), [1] * (amount - 1)
    while surplus > 0:
        candidates = [i for i in range(amount - 1) if counts[i] < limit]
        mass, budget = sum([loads[i] for i in candidates]), surplus
        for i in candidates:
            more = min(limit - counts[i], max(1, budget * loads[i] // mass), surplus)
            counts[i] = counts[i] + more
            surplus = surplus - more
    return np.array([limit] + counts)


def ragged(own_key, amount, total, reach, skew):
    if amount == 2:
        one = jax.random.randint(own_key, (), max(1, total - reach), min(reach, total - 1) + 1)
        return jnp.stack([one, total - one])
    sizes = jnp.asarray(profile(amount, total, reach, skew), jnp.int32)
    pairs = (amount - 1) // 2
    source_of, taker = sizes[1:1 + 2 * pairs:2], sizes[2:2 + 2 * pairs:2]
    slack = jnp.minimum(source_of - 1, reach - taker)
    moved = jax.random.randint(jax.random.fold_in(own_key, 1), (pairs,), 0, 1 << 20) % (slack + 1)
    sizes = sizes.at[1:1 + 2 * pairs:2].set(source_of - moved).at[2:2 + 2 * pairs:2].set(taker + moved)
    return sizes[jax.random.permutation(jax.random.fold_in(own_key, 2), amount)]


def scatter_about(key, dims, width, bound, cuts=(), kind=jnp.bfloat16):
    entries = width * jax.random.normal(key, dims, jnp.float32)
    if cuts:
        entries = entries * levels(key, dims, cuts, -0.22, 0.18)
    return jnp.clip(entries, -bound, bound).astype(kind)


def setup_inputs(seed: int = 0, part: int = 0) -> dict:
    seeds = jax.random.split(jax.random.key(seed), 10)
    part_keys = jax.random.split(jax.random.fold_in(seeds[9], part), 10)
    blocks = scatter_about(part_keys[0], (NITEMS, BA, BO, BO), 1.0, 6.0, ((0, 8), (2, 2)))
    occupied = scatter_about(part_keys[1], (NTAU, NO, NO), BO ** -0.5, 0.5, ((1, 16),))
    virtual = scatter_about(part_keys[2], (NTAU, NO, NO), BO ** -0.5, 0.5, ((1, 16),))
    item_mu = place_ends(jax.random.randint(part_keys[3], (NITEMS,), 0, NB), jax.random.fold_in(part_keys[3], 1), 0, NB - 1).astype(jnp.int32)
    item_nu = place_ends(jax.random.randint(part_keys[4], (NITEMS,), 0, NB), jax.random.fold_in(part_keys[4], 1), 0, NB - 1).astype(jnp.int32)
    item_target = place_ends(jax.random.randint(part_keys[5], (NITEMS,), 0, NT), jax.random.fold_in(part_keys[5], 1), 0, NT - 1).astype(jnp.int32)
    live_counts = ragged(part_keys[6], N_WIDE, LIVE_TOTAL, SLOTS, 2).astype(jnp.int32)
    target_occ = place_ends(jax.random.randint(part_keys[7], (NT,), 0, NB), jax.random.fold_in(part_keys[7], 1), 0, NB - 1).astype(jnp.int32)
    target_virt = place_ends(jax.random.randint(part_keys[8], (NT,), 0, NB), jax.random.fold_in(part_keys[8], 1), 0, NB - 1).astype(jnp.int32)
    return {"blocks": blocks, "occupied": occupied, "virtual": virtual, "item_mu": item_mu, "item_nu": item_nu, "item_target": item_target, "live_counts": live_counts, "target_occ": target_occ, "target_virt": target_virt}


def reference(blocks, occupied, virtual, item_mu, item_nu, item_target, live_counts, target_occ, target_virt):
    order = jnp.arange(NITEMS, dtype=jnp.int32)
    live = (order % SLOTS < live_counts[order // SLOTS]).astype(jnp.float32)
    zero_index = jnp.int32(0)

    def step(total, index):
        target = item_target[index]
        mu_block = item_mu[index]
        nu_block = item_nu[index]
        lam_block = target_occ[target]
        sig_block = target_virt[target]
        slab = blocks[index].astype(jnp.float32)
        virt_block = lax.dynamic_slice(virtual, (zero_index, (nu_block * BO).astype(jnp.int32), (sig_block * BO).astype(jnp.int32)), (NTAU, BO, BO)).astype(jnp.float32)
        occ_block = lax.dynamic_slice(occupied, (zero_index, (lam_block * BO).astype(jnp.int32), (mu_block * BO).astype(jnp.int32)), (NTAU, BO, BO)).astype(jnp.float32)
        half = jnp.einsum('pmn,tns->tpms', slab, virt_block).astype(jnp.bfloat16)
        term = jnp.einsum('tpms,tlm->tpsl', half.astype(jnp.float32), occ_block) * live[index]
        current = lax.dynamic_index_in_dim(total, target, 1, keepdims=False)
        total = lax.dynamic_update_index_in_dim(total, current + term, target, 1)
        return total, None

    start = jnp.zeros((NTAU, NT, BA, BO, BO), jnp.float32)
    total, unused = lax.scan(step, start, order)
    return total.astype(jnp.bfloat16)
```

```python
import functools

import jax
import jax.numpy as jnp
from jax import lax
from jax.experimental import pallas as pl
from jax.experimental.pallas import tpu as pltpu
from jax.sharding import PartitionSpec as P

MESH = pl.DeviceIdType.MESH
NT_DIMS = (((1,), (1,)), ((), ()))


def offset_of(turn, wide):
    sign = 1 - 2 * lax.rem(turn, 2)
    return wide // 2 + sign * lax.div(turn + 1, 2)


def exchange_kernel(
    wide, narrow, lag, blocks, gathered, own_sem, z_send, z_recv, x_send, x_recv, xo_send, xo_recv
):
    slots = blocks.shape[0]
    rows = gathered.shape[1]
    mrows = blocks.shape[2]
    me = lax.axis_index("wide")
    here = lax.axis_index("narrow")
    sends = slots * (wide - 1)

    barrier = pltpu.get_barrier_semaphore()

    def greet(step, carry):
        peer = lax.rem(me + step, wide)
        pl.semaphore_signal(barrier, inc=1, device_id={"wide": peer}, device_id_type=MESH)
        return carry

    lax.fori_loop(1, wide, greet, 0)
    for step in range(1, narrow):
        peer = lax.rem(here + step, narrow)
        pl.semaphore_signal(barrier, inc=1, device_id={"narrow": peer}, device_id_type=MESH)
    pl.semaphore_wait(barrier, wide - 1 + narrow - 1)

    columns = pl.ds(pl.multiple_of(here * mrows, mrows), mrows)

    def place(slot):
        return gathered.at[slot, :, columns, :]

    def rows_for(slot, device):
        return blocks.at[slot, pl.ds(device * rows, rows)]

    def z_copy(turn):
        slot = lax.div(turn, wide - 1)
        peer = lax.rem(me + offset_of(lax.rem(turn, wide - 1), wide), wide)
        return pltpu.make_async_remote_copy(
            src_ref=rows_for(slot, peer),
            dst_ref=place(me * slots + slot),
            send_sem=z_send.at[turn],
            recv_sem=z_recv.at[turn],
            device_id={"wide": peer},
            device_id_type=MESH,
        )

    def x_copy(turn, step):
        slot = lax.div(turn, wide - 1)
        offset = offset_of(lax.rem(turn, wide - 1), wide)
        source = lax.rem(me + wide - offset, wide)
        return pltpu.make_async_remote_copy(
            src_ref=place(source * slots + slot),
            dst_ref=place(source * slots + slot),
            send_sem=x_send.at[step - 1, turn],
            recv_sem=x_recv.at[step - 1, turn],
            device_id={"narrow": lax.rem(here + step, narrow)},
            device_id_type=MESH,
        )

    def own_x_copy(slot, step):
        return pltpu.make_async_remote_copy(
            src_ref=rows_for(slot, me),
            dst_ref=place(me * slots + slot),
            send_sem=xo_send.at[step - 1, slot],
            recv_sem=xo_recv.at[step - 1, slot],
            device_id={"narrow": lax.rem(here + step, narrow)},
            device_id_type=MESH,
        )

    def own_copy(slot):
        return pltpu.make_async_copy(
            rows_for(slot, me), place(me * slots + slot), own_sem.at[slot]
        )

    def begin(turn, carry):
        z_copy(turn).start()
        return carry

    def forward(turn, carry):
        z_copy(turn).wait_recv()
        for step in range(1, narrow):
            x_copy(turn, step).start()
        return carry

    def both(turn, carry):
        begin(turn, carry)
        return forward(turn - lag, carry)

    lax.fori_loop(0, lag, begin, 0)
    for slot in range(slots):
        for step in range(1, narrow):
            own_x_copy(slot, step).start()
        own_copy(slot).start()
    lax.fori_loop(lag, sends, both, 0)
    lax.fori_loop(sends - lag, sends, forward, 0)

    def finish(turn, carry):
        z_copy(turn).wait_send()
        for step in range(1, narrow):
            x_copy(turn, step).wait()
        return carry

    for slot in range(slots):
        own_copy(slot).wait()
        for step in range(1, narrow):
            own_x_copy(slot, step).wait()
    lax.fori_loop(0, sends, finish, 0)


def exchange(blocks):
    slots, aux, mrows, width = blocks.shape
    wide = lax.axis_size("wide")
    narrow = lax.axis_size("narrow")
    sends = slots * (wide - 1)
    return pl.pallas_call(
        functools.partial(exchange_kernel, wide, narrow, min(4, sends)),
        out_shape=jax.ShapeDtypeStruct(
            (wide * slots, aux // wide, narrow * mrows, width), blocks.dtype
        ),
        in_specs=[pl.BlockSpec(memory_space=pl.ANY)],
        out_specs=pl.BlockSpec(memory_space=pl.ANY),
        scratch_shapes=[
            pltpu.SemaphoreType.DMA((slots,)),
            pltpu.SemaphoreType.DMA((sends,)),
            pltpu.SemaphoreType.DMA((sends,)),
            pltpu.SemaphoreType.DMA((narrow - 1, sends)),
            pltpu.SemaphoreType.DMA((narrow - 1, sends)),
            pltpu.SemaphoreType.DMA((narrow - 1, slots)),
            pltpu.SemaphoreType.DMA((narrow - 1, slots)),
        ],
        compiler_params=pltpu.CompilerParams(collective_id=0, has_side_effects=True),
        name="exchange",
    )(blocks)


def contract_kernel(meta, x_ref, virt_ref, occ_ref, out_ref, total, half):
    turn = pl.program_id(0)
    times, rows, sigma, width = total.shape
    kind = meta[2, turn]
    occ_row = pl.multiple_of(meta[3, turn] * width, width)
    occ_column = pl.multiple_of(meta[4, turn] * width, width)
    virt_row = pl.multiple_of(meta[5, turn] * sigma, sigma)
    virt_column = pl.multiple_of(meta[6, turn] * width, width)

    @pl.when(kind == 4)
    def _():
        out_ref[...] = jnp.zeros_like(out_ref)

    @pl.when(kind < 4)
    def _():
        virt = jnp.concatenate(
            [
                virt_ref[time, pl.ds(virt_row, sigma), pl.ds(virt_column, width)]
                for time in range(times)
            ],
            axis=0,
        )
        for row in range(0, rows, 2):
            pair = x_ref[0, row : row + 2].reshape(2 * width, width)
            product = lax.dot_general(
                virt, pair, NT_DIMS, preferred_element_type=jnp.float32
            ).astype(jnp.bfloat16)
            half[:, row] = product[:, :width].reshape(times, sigma, width)
            half[:, row + 1] = product[:, width:].reshape(times, sigma, width)

    def second(first, last):
        def step(time, carry):
            occ = occ_ref[time, pl.ds(occ_row, width), pl.ds(occ_column, width)]
            term = lax.dot_general(
                half[time].reshape(rows * sigma, width),
                occ,
                NT_DIMS,
                preferred_element_type=jnp.float32,
            ).reshape(rows, sigma, width)
            if not first:
                term = term + total[time]
            if last:
                out_ref[time, 0] = term.astype(out_ref.dtype)
            else:
                total[time] = term
            return carry

        lax.fori_loop(0, times, step, 0, unroll=2)

    for code in range(4):

        @pl.when(kind == code)
        def _(code=code):
            second(code % 2 == 1, code // 2 == 1)


def contract(meta, gathered, virt, occ, targets):
    items, rows, width, _ = gathered.shape
    times = occ.shape[0]
    sigma = virt.shape[1] // (virt.shape[2] // width)
    per_item = 4 * times * rows * sigma * width * width
    grid_spec = pltpu.PrefetchScalarGridSpec(
        num_scalar_prefetch=1,
        grid=(meta.shape[1],),
        in_specs=[
            pl.BlockSpec((1, rows, width, width), lambda j, meta: (meta[0, j], 0, 0, 0)),
            pl.BlockSpec(virt.shape, lambda j, meta: (0, 0, 0)),
            pl.BlockSpec(occ.shape, lambda j, meta: (0, 0, 0)),
        ],
        out_specs=pl.BlockSpec(
            (times, 1, rows, sigma, width), lambda j, meta: (0, meta[1, j], 0, 0, 0)
        ),
        scratch_shapes=[
            pltpu.VMEM((times, rows, sigma, width), jnp.float32),
            pltpu.VMEM((times, rows, sigma, width), jnp.bfloat16),
        ],
    )
    return pl.pallas_call(
        contract_kernel,
        grid_spec=grid_spec,
        out_shape=jax.ShapeDtypeStruct((times, targets, rows, sigma, width), jnp.bfloat16),
        compiler_params=pltpu.CompilerParams(
            dimension_semantics=("arbitrary",), vmem_limit_bytes=48 * 1024 * 1024
        ),
        cost_estimate=pl.CostEstimate(
            flops=per_item * items,
            bytes_accessed=2 * times * targets * rows * sigma * width + 2 * gathered.size,
            transcendentals=0,
        ),
        name="contract",
    )(meta, gathered, virt, occ)


def work_list(lists, slots, target_occ, target_virt):
    mu, nu, target = (lists[:, k * slots : (k + 1) * slots].reshape(-1) for k in range(3))
    items = target.shape[0]
    targets = target_occ.shape[0]
    live = (jnp.arange(slots)[None, :] < lists[:, 3 * slots :]).reshape(-1)
    names = jnp.arange(targets, dtype=jnp.int32)
    named = jnp.any((target[None, :] == names[:, None]) & live[None, :], axis=1)
    valid = jnp.concatenate([live, ~named])
    key = jnp.concatenate([target, names])
    order = jnp.arange(items + targets, dtype=jnp.int32)
    same = valid[None, :] & (key[None, :] == key[:, None])
    ahead = order[None, :] < order[:, None]
    first = ~jnp.any(same & ahead, axis=1)
    last = ~jnp.any(same & (order[None, :] > order[:, None]), axis=1)
    before = valid[None, :] & ((key[None, :] < key[:, None]) | (same & ahead))
    rank = jnp.sum(before, axis=1, dtype=jnp.int32)
    blank = jnp.zeros((targets,), jnp.int32)
    is_item = order < items
    kind = jnp.where(is_item, first.astype(jnp.int32) + 2 * last.astype(jnp.int32), 4)
    at_target = key[:, None] == names[None, :]
    lam = jnp.sum(jnp.where(at_target, target_occ[None, :], 0), axis=1)
    sig = jnp.sum(jnp.where(at_target, target_virt[None, :], 0), axis=1)
    table = jnp.stack(
        [
            jnp.where(is_item, order, 0),
            key,
            kind,
            lam,
            jnp.concatenate([mu, blank]),
            sig,
            jnp.concatenate([nu, blank]),
        ]
    )
    steps = jnp.sum(valid, dtype=jnp.int32)
    chosen = valid[None, :] & (rank[None, :] == jnp.minimum(order, steps - 1)[:, None])
    meta = jnp.sum(jnp.where(chosen[None], table[:, None, :], 0), axis=2, dtype=jnp.int32)
    return meta.at[2].set(jnp.where(order < steps, meta[2], 5))


def local(
    blocks, occupied, virtual, item_mu, item_nu, item_target, live_counts, target_occ, target_virt
):
    slots = blocks.shape[0]
    width = blocks.shape[3]
    narrow = lax.axis_size("narrow")
    sigma = width // narrow
    own = jnp.concatenate([item_mu, item_nu, item_target, live_counts])
    lists = lax.all_gather(own, "wide", axis=0, tiled=False)
    times, _, across = virtual.shape
    virt = virtual.reshape(times, -1, across // width, narrow, sigma)
    virt = lax.all_to_all(virt, "narrow", split_axis=3, concat_axis=1, tiled=True)
    virt = virt.reshape(times, -1, across // narrow)
    virt = lax.all_gather(virt, "wide", axis=1, tiled=True)
    occ = lax.all_gather(occupied, "wide", axis=1, tiled=False)
    occ = lax.all_gather(occ, "narrow", axis=2, tiled=False)
    occ = occ.reshape(times, -1, across)
    virt = virt.transpose(0, 2, 1)
    meta = work_list(lists, slots, target_occ, target_virt)
    gathered = exchange(blocks)
    return contract(meta, gathered, virt, occ, target_occ.shape[0])


def solution(mesh):
    in_specs = (
        P(("groups", "wide"), None, "narrow", None),
        P("groups", ("wide", "narrow"), None),
        P("groups", ("wide", "narrow"), None),
        P(("groups", "wide")),
        P(("groups", "wide")),
        P(("groups", "wide")),
        P(("groups", "wide")),
        P("groups"),
        P("groups"),
    )
    out_specs = P("groups", None, "wide", "narrow", None)
    return jax.shard_map(local, mesh=mesh, in_specs=in_specs, out_specs=out_specs, check_vma=False)
```

```python
import functools

import jax
import jax.numpy as jnp
from jax import lax
from jax.experimental import pallas as pl
from jax.experimental.pallas import tpu as pltpu
from jax.sharding import PartitionSpec as P

MESH = pl.DeviceIdType.MESH
NT_DIMS = (((1,), (1,)), ((), ()))


def offset_of(turn, wide):
    sign = 1 - 2 * lax.rem(turn, 2)
    return wide // 2 + sign * lax.div(turn + 1, 2)


def exchange_kernel(
    wide, narrow, lag, blocks, gathered, own_sem, z_send, z_recv, x_send, x_recv, xo_send, xo_recv
):
    slots = blocks.shape[0]
    rows = gathered.shape[1]
    mrows = blocks.shape[2]
    me = lax.axis_index("wide")
    here = lax.axis_index("narrow")
    sends = slots * (wide - 1)

    barrier = pltpu.get_barrier_semaphore()

    def greet(step, carry):
        peer = lax.rem(me + step, wide)
        pl.semaphore_signal(barrier, inc=1, device_id={"wide": peer}, device_id_type=MESH)
        return carry

    lax.fori_loop(1, wide, greet, 0)
    for step in range(1, narrow):
        peer = lax.rem(here + step, narrow)
        pl.semaphore_signal(barrier, inc=1, device_id={"narrow": peer}, device_id_type=MESH)
    pl.semaphore_wait(barrier, wide - 1 + narrow - 1)

    columns = pl.ds(pl.multiple_of(here * mrows, mrows), mrows)

    def place(slot):
        return gathered.at[slot, :, columns, :]

    def rows_for(slot, device):
        return blocks.at[slot, pl.ds(device * rows, rows)]

    def z_copy(turn):
        slot = lax.div(turn, wide - 1)
        peer = lax.rem(me + offset_of(lax.rem(turn, wide - 1), wide), wide)
        return pltpu.make_async_remote_copy(
            src_ref=rows_for(slot, peer),
            dst_ref=place(me * slots + slot),
            send_sem=z_send.at[turn],
            recv_sem=z_recv.at[turn],
            device_id={"wide": peer},
            device_id_type=MESH,
        )

    def x_copy(turn, step):
        slot = lax.div(turn, wide - 1)
        offset = offset_of(lax.rem(turn, wide - 1), wide)
        source = lax.rem(me + wide - offset, wide)
        return pltpu.make_async_remote_copy(
            src_ref=place(source * slots + slot),
            dst_ref=place(source * slots + slot),
            send_sem=x_send.at[step - 1, turn],
            recv_sem=x_recv.at[step - 1, turn],
            device_id={"narrow": lax.rem(here + step, narrow)},
            device_id_type=MESH,
        )

    def own_x_copy(slot, step):
        return pltpu.make_async_remote_copy(
            src_ref=rows_for(slot, me),
            dst_ref=place(me * slots + slot),
            send_sem=xo_send.at[step - 1, slot],
            recv_sem=xo_recv.at[step - 1, slot],
            device_id={"narrow": lax.rem(here + step, narrow)},
            device_id_type=MESH,
        )

    def own_copy(slot):
        return pltpu.make_async_copy(
            rows_for(slot, me), place(me * slots + slot), own_sem.at[slot]
        )

    def begin(turn, carry):
        z_copy(turn).start()
        return carry

    def forward(turn, carry):
        z_copy(turn).wait_recv()
        for step in range(1, narrow):
            x_copy(turn, step).start()
        return carry

    def both(turn, carry):
        begin(turn, carry)
        return forward(turn - lag, carry)

    lax.fori_loop(0, lag, begin, 0)
    for slot in range(slots):
        for step in range(1, narrow):
            own_x_copy(slot, step).start()
        own_copy(slot).start()
    lax.fori_loop(lag, sends, both, 0)
    lax.fori_loop(sends - lag, sends, forward, 0)

    def finish(turn, carry):
        z_copy(turn).wait_send()
        for step in range(1, narrow):
            x_copy(turn, step).wait()
        return carry

    for slot in range(slots):
        own_copy(slot).wait()
        for step in range(1, narrow):
            own_x_copy(slot, step).wait()
    lax.fori_loop(0, sends, finish, 0)


def exchange(blocks):
    slots, aux, mrows, width = blocks.shape
    wide = lax.axis_size("wide")
    narrow = lax.axis_size("narrow")
    sends = slots * (wide - 1)
    return pl.pallas_call(
        functools.partial(exchange_kernel, wide, narrow, min(4, sends)),
        out_shape=jax.ShapeDtypeStruct(
            (wide * slots, aux // wide, narrow * mrows, width), blocks.dtype
        ),
        in_specs=[pl.BlockSpec(memory_space=pl.ANY)],
        out_specs=pl.BlockSpec(memory_space=pl.ANY),
        scratch_shapes=[
            pltpu.SemaphoreType.DMA((slots,)),
            pltpu.SemaphoreType.DMA((sends,)),
            pltpu.SemaphoreType.DMA((sends,)),
            pltpu.SemaphoreType.DMA((narrow - 1, sends)),
            pltpu.SemaphoreType.DMA((narrow - 1, sends)),
            pltpu.SemaphoreType.DMA((narrow - 1, slots)),
            pltpu.SemaphoreType.DMA((narrow - 1, slots)),
        ],
        compiler_params=pltpu.CompilerParams(collective_id=0, has_side_effects=True),
        name="exchange",
    )(blocks)


def contract_kernel(meta, x_ref, virt_ref, occ_ref, out_ref, total, half):
    turn = pl.program_id(0)
    times, rows, sigma, width = total.shape
    kind = meta[2, turn]
    occ_row = pl.multiple_of(meta[3, turn] * width, width)
    occ_column = pl.multiple_of(meta[4, turn] * width, width)
    virt_row = pl.multiple_of(meta[5, turn] * sigma, sigma)
    virt_column = pl.multiple_of(meta[6, turn] * width, width)

    @pl.when(kind == 4)
    def _():
        out_ref[...] = jnp.zeros_like(out_ref)

    @pl.when(kind < 4)
    def _():
        virt = jnp.concatenate(
            [
                virt_ref[time, pl.ds(virt_row, sigma), pl.ds(virt_column, width)]
                for time in range(times)
            ],
            axis=0,
        )
        for row in range(0, rows, 2):
            pair = x_ref[0, row : row + 2].reshape(2 * width, width)
            product = lax.dot_general(
                virt, pair, NT_DIMS, preferred_element_type=jnp.float32
            ).astype(jnp.bfloat16)
            half[:, row] = product[:, :width].reshape(times, sigma, width)
            half[:, row + 1] = product[:, width:].reshape(times, sigma, width)

    def second(first, last):
        def step(time, carry):
            occ = occ_ref[time, pl.ds(occ_row, width), pl.ds(occ_column, width)]
            term = lax.dot_general(
                half[time].reshape(rows * sigma, width),
                occ,
                NT_DIMS,
                preferred_element_type=jnp.float32,
            ).reshape(rows, sigma, width)
            if not first:
                term = term + total[time]
            if last:
                out_ref[time, 0] = term.astype(out_ref.dtype)
            else:
                total[time] = term
            return carry

        lax.fori_loop(0, times, step, 0, unroll=2)

    for code in range(4):

        @pl.when(kind == code)
        def _(code=code):
            second(code % 2 == 1, code // 2 == 1)


def contract(meta, gathered, virt, occ, targets):
    items, rows, width, _ = gathered.shape
    times = occ.shape[0]
    sigma = virt.shape[1] // (virt.shape[2] // width)
    per_item = 4 * times * rows * sigma * width * width
    grid_spec = pltpu.PrefetchScalarGridSpec(
        num_scalar_prefetch=1,
        grid=(meta.shape[1],),
        in_specs=[
            pl.BlockSpec((1, rows, width, width), lambda j, meta: (meta[0, j], 0, 0, 0)),
            pl.BlockSpec(virt.shape, lambda j, meta: (0, 0, 0)),
            pl.BlockSpec(occ.shape, lambda j, meta: (0, 0, 0)),
        ],
        out_specs=pl.BlockSpec(
            (times, 1, rows, sigma, width), lambda j, meta: (0, meta[1, j], 0, 0, 0)
        ),
        scratch_shapes=[
            pltpu.VMEM((times, rows, sigma, width), jnp.float32),
            pltpu.VMEM((times, rows, sigma, width), jnp.bfloat16),
        ],
    )
    return pl.pallas_call(
        contract_kernel,
        grid_spec=grid_spec,
        out_shape=jax.ShapeDtypeStruct((times, targets, rows, sigma, width), jnp.bfloat16),
        compiler_params=pltpu.CompilerParams(
            dimension_semantics=("arbitrary",), vmem_limit_bytes=48 * 1024 * 1024
        ),
        cost_estimate=pl.CostEstimate(
            flops=per_item * items,
            bytes_accessed=2 * times * targets * rows * sigma * width + 2 * gathered.size,
            transcendentals=0,
        ),
        name="contract",
    )(meta, gathered, virt, occ)


def work_list(lists, slots, target_occ, target_virt):
    mu, nu, target = (lists[:, k * slots : (k + 1) * slots].reshape(-1) for k in range(3))
    items = target.shape[0]
    targets = target_occ.shape[0]
    live = (jnp.arange(slots)[None, :] < lists[:, 3 * slots :]).reshape(-1)
    names = jnp.arange(targets, dtype=jnp.int32)
    named = jnp.any((target[None, :] == names[:, None]) & live[None, :], axis=1)
    valid = jnp.concatenate([live, ~named])
    key = jnp.concatenate([target, names])
    order = jnp.arange(items + targets, dtype=jnp.int32)
    same = valid[None, :] & (key[None, :] == key[:, None])
    ahead = order[None, :] < order[:, None]
    first = ~jnp.any(same & ahead, axis=1)
    last = ~jnp.any(same & (order[None, :] > order[:, None]), axis=1)
    before = valid[None, :] & ((key[None, :] < key[:, None]) | (same & ahead))
    rank = jnp.sum(before, axis=1, dtype=jnp.int32)
    blank = jnp.zeros((targets,), jnp.int32)
    is_item = order < items
    kind = jnp.where(is_item, first.astype(jnp.int32) + 2 * last.astype(jnp.int32), 4)
    at_target = key[:, None] == names[None, :]
    lam = jnp.sum(jnp.where(at_target, target_occ[None, :], 0), axis=1)
    sig = jnp.sum(jnp.where(at_target, target_virt[None, :], 0), axis=1)
    table = jnp.stack(
        [
            jnp.where(is_item, order, 0),
            key,
            kind,
            lam,
            jnp.concatenate([mu, blank]),
            sig,
            jnp.concatenate([nu, blank]),
        ]
    )
    steps = jnp.sum(valid, dtype=jnp.int32)
    chosen = valid[None, :] & (rank[None, :] == jnp.minimum(order, steps - 1)[:, None])
    meta = jnp.sum(jnp.where(chosen[None], table[:, None, :], 0), axis=2, dtype=jnp.int32)
    return meta.at[2].set(jnp.where(order < steps, meta[2], 5))


def local(
    blocks, occupied, virtual, item_mu, item_nu, item_target, live_counts, target_occ, target_virt
):
    slots = blocks.shape[0]
    width = blocks.shape[3]
    narrow = lax.axis_size("narrow")
    sigma = width // narrow
    own = jnp.concatenate([item_mu, item_nu, item_target, live_counts])
    lists = lax.all_gather(own, "wide", axis=0, tiled=False)
    times, _, across = virtual.shape
    virt = virtual.reshape(times, -1, across // width, narrow, sigma)
    virt = lax.all_to_all(virt, "narrow", split_axis=3, concat_axis=1, tiled=True)
    virt = virt.reshape(times, -1, across // narrow)
    virt = lax.all_gather(virt, "wide", axis=1, tiled=True)
    occ = lax.all_gather(occupied, ("wide", "narrow"), axis=1, tiled=True)
    virt = virt.transpose(0, 2, 1)
    meta = work_list(lists, slots, target_occ, target_virt)
    gathered = exchange(blocks)
    return contract(meta, gathered, virt, occ, target_occ.shape[0])


def solution(mesh):
    in_specs = (
        P(("groups", "wide"), None, "narrow", None),
        P("groups", ("wide", "narrow"), None),
        P("groups", ("wide", "narrow"), None),
        P(("groups", "wide")),
        P(("groups", "wide")),
        P(("groups", "wide")),
        P(("groups", "wide")),
        P("groups"),
        P("groups"),
    )
    out_specs = P("groups", None, "wide", "narrow", None)
    return jax.shard_map(local, mesh=mesh, in_specs=in_specs, out_specs=out_specs, check_vma=False)
```
